512 devices in a mesh: ctx: 128 (over z, x, core), tp: 4 (over y).
Axes of the slice: x: 4, y: 4, z: 16, core: 2. Of those that a mesh axis runs over, the one named last changes fastest.
Arguments:
- queries: bfloat16 [32768, 1024], P('ctx', 'tp'), may hold values from -6 to 6
- keys: bfloat16 [32768, 1024], P('ctx', 'tp'), may hold values from -6 to 6
- values: bfloat16 [32768, 1024], P('ctx', 'tp'), may hold values from -20 to 20, as said below
- gain: float32 [1024], P('tp'), may hold values from 0.25 to 1.75
- out_grad: bfloat16 [32768, 1024], P('ctx', 'tp'), may hold values from -6 to 6
Outputs:
- normed: bfloat16 [32768, 1024], P('ctx', 'tp')
- grad_queries: bfloat16 [32768, 1024], P('ctx', 'tp')
- grad_keys: bfloat16 [32768, 1024], P('ctx', 'tp')
- grad_values: bfloat16 [32768, 1024], P('ctx', 'tp')
The draws below stay inside these ranges and needn't reach their ends.
Inputs may be any that keep to these rules, and one draw needn't show every extreme that they name: values of order one, each head at its own scale.
All inputs are finite; a program needn't handle non-finite values.
Results may differ from the reference program's by a relative error of at most 0.0065.
Values sent between devices are 32-bit elements; how exact they have to be, the bound alone decides.
A program may use at most 64 MiB of HBM per device.

```python
import jax
import jax.numpy as jnp
from jax import lax

HEAD = 128
TOK_DEV = 256
HEADS = 8
SEQ = 32768
N_CTX = 128


def draw_values(key, part):
    key = jax.random.fold_in(key, 5)
    jitter_key, main_key = jax.random.split(key)
    placing = (jnp.arange(HEADS, dtype=jnp.float32) + jax.random.uniform(jitter_key, (HEADS,), jnp.float32)) / HEADS
    scales = 10.0 ** (placing - 0.5)
    noise = jnp.clip(jax.random.normal(main_key, (SEQ, HEADS, HEAD), jnp.float32), -6.0, 6.0)
    return (noise * scales[None, :, None]).reshape(SEQ, HEADS * HEAD).astype(jnp.bfloat16)


def steps_of(own_key, shape, cuts, least, largest):
    loudness = 1.0
    for dim, blocks in cuts:
        heights = jax.random.uniform(jax.random.fold_in(jax.random.fold_in(own_key, 6), dim), (blocks,), jnp.float32, least / len(cuts), largest / len(cuts))
        loudness = loudness * jnp.repeat(jnp.exp(heights), shape[dim] // blocks).reshape((-1,) + (1,) * (len(shape) - 1 - dim))
    return loudness


def scatter_about(rng, dims, width, most, pieces=(), held_as=jnp.bfloat16):
    result = width * jax.random.normal(rng, dims, jnp.float32)
    if pieces:
        result = result * steps_of(rng, dims, pieces, -0.22, 0.18)
    return jnp.clip(result, -most, most).astype(held_as)


def setup_inputs(seed: int = 0) -> dict:
    streams_of = jax.random.split(jax.random.key(seed), 6)
    return {
        "queries": scatter_about(streams_of[0], (SEQ, HEADS * HEAD), 1.0, 6.0, ((0, 128), (1, 4))),
        "keys": scatter_about(streams_of[1], (SEQ, HEADS * HEAD), 1.0, 6.0, ((0, 128), (1, 4))),
        "values": draw_values(jax.random.fold_in(streams_of[5], 71), 0),
        "gain": jnp.clip(1.0 + 0.15 * jax.random.normal(streams_of[3], (HEADS * HEAD,), jnp.float32), 0.25, 1.75),
        "out_grad": scatter_about(streams_of[4], (SEQ, HEADS * HEAD), 1.0, 6.0, ((0, 128), (1, 4))),
    }


epsilon = 1e-06

def reference(queries, keys, values, gain, out_grad):
    blocks = N_CTX
    tokens = TOK_DEV
    factor = (HEAD * SEQ) ** (-0.5)
    features = HEADS * HEAD
    q_all = queries.reshape(blocks, tokens, HEADS, HEAD)
    k_all = keys.reshape(blocks, tokens, HEADS, HEAD)
    v_all = values.reshape(blocks, tokens, HEADS, HEAD)
    position = jnp.arange(tokens, dtype=jnp.int32)
    causal = position[:, None] >= position[None, :]

    def make_scores(q_blk, k_blk):
        raw = jnp.einsum('thd,shd->hts', q_blk.astype(jnp.float32), k_blk.astype(jnp.float32)) * factor
        return jnp.where(causal[None], raw, 0.0).astype(jnp.bfloat16)

    def forward(carry, blk):
        q_blk, k_blk, v_blk = blk
        prefix = carry.astype(jnp.bfloat16)
        scores = make_scores(q_blk, k_blk)
        attended = factor * jnp.einsum('thd,hde->the', q_blk.astype(jnp.float32), prefix.astype(jnp.float32))
        attended = attended + jnp.einsum('hts,she->the', scores.astype(jnp.float32), v_blk.astype(jnp.float32))
        states = jnp.einsum('thd,the->hde', k_blk.astype(jnp.float32), v_blk.astype(jnp.float32))
        return (carry + states, (attended, prefix))
    start = jnp.zeros((HEADS, HEAD, HEAD), jnp.float32)
    _, (attended, prefixes) = lax.scan(forward, start, (q_all, k_all, v_all))
    inv_rms = lax.rsqrt(lax.optimization_barrier(jnp.sum(attended * attended, axis=(2, 3))) / features + epsilon)
    gains = gain.astype(jnp.float32).reshape(HEADS, HEAD)
    normed = (attended * inv_rms[:, :, None, None] * gains).reshape(SEQ, features).astype(jnp.bfloat16)
    weighted = out_grad.astype(jnp.float32).reshape(blocks, tokens, HEADS, HEAD) * gains
    row_mean = lax.optimization_barrier(jnp.sum(weighted * attended, axis=(2, 3))) / features
    grad_attn = inv_rms[:, :, None, None] * (weighted - attended * (inv_rms * inv_rms * row_mean)[:, :, None, None])
    grad_attn = grad_attn.astype(jnp.bfloat16)

    def backward(carry, blk):
        q_blk, k_blk, v_blk, g_blk, prefix = blk
        suffix = carry.astype(jnp.bfloat16)
        qf = q_blk.astype(jnp.float32)
        kf = k_blk.astype(jnp.float32)
        vf = v_blk.astype(jnp.float32)
        gf = g_blk.astype(jnp.float32)
        pf = prefix.astype(jnp.float32)
        sf = suffix.astype(jnp.float32)
        scores = make_scores(q_blk, k_blk).astype(jnp.float32)
        raw = jnp.einsum('the,she->hts', gf, vf) * factor
        grad_scores = jnp.where(causal[None], raw, 0.0).astype(jnp.bfloat16).astype(jnp.float32)
        grad_q = factor * jnp.einsum('the,hde->thd', gf, pf) + jnp.einsum('hts,shd->thd', grad_scores, kf)
        grad_k = factor * jnp.einsum('the,hde->thd', vf, sf) + jnp.einsum('hts,thd->shd', grad_scores, qf)
        grad_v = factor * jnp.einsum('thd,hde->the', kf, sf) + jnp.einsum('hts,the->she', scores, gf)
        updates = jnp.einsum('thd,the->hde', qf, gf)
        return (carry + updates, (grad_q.astype(jnp.bfloat16), grad_k.astype(jnp.bfloat16), grad_v.astype(jnp.bfloat16)))
    _, (grad_q, grad_k, grad_v) = lax.scan(backward, start, (q_all, k_all, v_all, grad_attn, prefixes), reverse=True)
    return (normed, grad_q.reshape(SEQ, features), grad_k.reshape(SEQ, features), grad_v.reshape(SEQ, features))
```

```python
import functools

import jax
import jax.numpy as jnp
from jax import lax
from jax.experimental import pallas as pl
from jax.experimental.pallas import tpu as pltpu
from jax.sharding import PartitionSpec as P

HEAD = 128
GROUP = 16
EPSILON = 1e-06
MESH = pl.DeviceIdType.MESH
F32 = jnp.float32
BF16 = jnp.bfloat16

STEPS = sorted(
    [(dz, dx, dc) for dz in range(2) for dx in range(4) for dc in range(2) if (dz, dx, dc) != (0, 0, 0)],
    key=lambda s: -(s[0] + min(s[1], 4 - s[1]) + 0.1 * s[2]),
)


def dot(a, b):
    return lax.dot_general(a, b, (((1,), (0,)), ((), ())), preferred_element_type=F32)


def dot_t(a, b):
    return lax.dot_general(a, b, (((1,), (1,)), ((), ())), preferred_element_type=F32)


def core_kernel(
    n_ctx, n_tp,
    q_hbm, k_hbm, v_hbm, gain_ref, og_hbm,
    normed_hbm, gq_hbm, gk_hbm, gv_hbm,
    q, k, v, og,
    part, got, total, others, before, scan_out,
    rows_out, rows_in,
    q_t, v_t, w_t, local_t, att_t, scores_t, ga_t,
    gk_part, gv_part, obuf,
    in_sem, out_sem, send1, recv1, send2, recv2, send3, recv3, send_tp, recv_tp,
):
    ctx = lax.axis_index("ctx")
    tp = lax.axis_index("tp")
    n_groups = n_ctx // GROUP
    group = ctx // GROUP
    member = ctx % GROUP
    half, x, core = member // 8, (member // 2) % 4, member % 2
    tokens, width = q.shape
    heads = width // HEAD
    slice_rows = part.shape[2]
    factor = (HEAD * tokens * n_ctx) ** (-0.5)
    features = width * n_tp

    loads = [
        pltpu.make_async_copy(src, dst, in_sem.at[i])
        for i, (src, dst) in enumerate(((k_hbm, k), (v_hbm, v), (q_hbm, q), (og_hbm, og)))
    ]
    for load in loads:
        load.start()
    others[...] = jnp.zeros_like(others)

    def member_at(step):
        dz, dx, dc = step
        return ((half + dz) % 2) * 8 + ((x + dx) % 4) * 2 + (core + dc) % 2

    barrier = pltpu.get_barrier_semaphore()
    for d in range(1, n_groups):
        pl.semaphore_signal(
            barrier, inc=1, device_id=(((group + d) % n_groups) * GROUP + member, tp), device_id_type=MESH
        )
    for step in STEPS:
        pl.semaphore_signal(
            barrier, inc=1, device_id=(group * GROUP + member_at(step), tp), device_id_type=MESH
        )
    for d in range(1, n_tp):
        pl.semaphore_signal(barrier, inc=1, device_id=(ctx, (tp + d) % n_tp), device_id_type=MESH)

    row = lax.broadcasted_iota(jnp.int32, (tokens, tokens), 0)
    col = lax.broadcasted_iota(jnp.int32, (tokens, tokens), 1)
    causal_t = row <= col

    def cols(h):
        return pl.ds(h * HEAD, HEAD)

    def put_state(i, h, value):
        per = HEAD // slice_rows
        part[i, h * per:(h + 1) * per] = value.reshape(per, slice_rows, HEAD)

    def state_of(i, h):
        per = HEAD // slice_rows
        return scan_out[i, h * per:(h + 1) * per].reshape(HEAD, HEAD).astype(BF16)

    loads[0].wait()
    loads[1].wait()
    v_t[...] = v[...].T
    for h in range(heads):
        put_state(0, h, dot(v_t[cols(h), :], k[:, cols(h)]))
    loads[2].wait()
    q_t[...] = (q[...].astype(F32) * factor).astype(BF16).T
    loads[3].wait()

    pl.semaphore_wait(barrier, (GROUP - 1) + (n_groups - 1) + (n_tp - 1))

    def to_members(i, src, dst, send, recv):
        copies = []
        for step in STEPS:
            peer = member_at(step)
            copy = pltpu.make_async_remote_copy(
                src_ref=src.at[i, peer],
                dst_ref=dst.at[i, member],
                send_sem=send.at[i],
                recv_sem=recv.at[i],
                device_id=(group * GROUP + peer, tp),
                device_id_type=MESH,
            )
            copy.start()
            copies.append(copy)
        dst[i, pl.ds(member, 1)] = src[i, pl.ds(member, 1)]

    def members_all(i, src, dst, send, recv):
        most = pl.ds(0, GROUP - 1)
        return pltpu.make_async_remote_copy(
            src_ref=src.at[i, most],
            dst_ref=dst.at[i, most],
            send_sem=send.at[i],
            recv_sem=recv.at[i],
            device_id=(ctx, tp),
            device_id_type=MESH,
        )

    def group_copy(i, other):
        return pltpu.make_async_remote_copy(
            src_ref=total.at[i],
            dst_ref=others.at[i, group],
            send_sem=send2.at[i, other],
            recv_sem=recv2.at[i, group],
            device_id=(other * GROUP + member, tp),
            device_id_type=MESH,
        )

    def group_wait(i, other):
        return pltpu.make_async_remote_copy(
            src_ref=total.at[i],
            dst_ref=others.at[i, other],
            send_sem=send2.at[i, other],
            recv_sem=recv2.at[i, other],
            device_id=(other * GROUP + member, tp),
            device_id_type=MESH,
        )

    def scan_start(i):
        to_members(i, part, got, send1, recv1)

    def scan_middle(i):
        members_all(i, part, got, send1, recv1).wait_recv()
        acc = jnp.zeros((slice_rows, HEAD), F32)
        for s in range(GROUP):
            m = s if i == 0 else GROUP - 1 - s
            before[i, m] = acc
            acc = acc + got[i, m]
        total[i] = acc
        for d in range(n_groups - 1, 0, -1):
            other = group + d if i == 0 else group - d

            @pl.when(other < n_groups if i == 0 else other >= 0)
            def _():
                group_copy(i, other).start()

    def scan_end(i):
        for other in range(n_groups):

            @pl.when(other < group if i == 0 else other > group)
            def _():
                group_wait(i, other).wait_recv()

        carried = others[i, 0]
        for other in range(1, n_groups):
            carried = carried + others[i, other]
        before[i] = before[i] + carried[None]
        to_members(i, before, scan_out, send3, recv3)

    def scan_wait(i):
        members_all(i, before, scan_out, send3, recv3).wait_recv()

    scan_start(0)
    w_t[...] = (og[...].astype(F32) * gain_ref[...]).T
    for h in range(heads):
        raw = dot(k[:, cols(h)], q_t[cols(h), :])
        scores_t[h] = jnp.where(causal_t, raw, 0.0).astype(BF16)
    scan_middle(0)
    for h in range(heads):
        local_t[cols(h), :] = dot(v_t[cols(h), :], scores_t[h])
    scan_end(0)
    scan_wait(0)

    power = jnp.zeros((1, tokens), F32)
    row_total = jnp.zeros((1, tokens), F32)
    for h in range(heads):
        att = dot(state_of(0, h), q_t[cols(h), :]) + local_t[cols(h), :]
        att_t[cols(h), :] = att
        power = power + jnp.sum(att * att, axis=0, keepdims=True)
        row_total = row_total + jnp.sum(w_t[cols(h), :] * att, axis=0, keepdims=True)
    rows_out[0:1, :] = power
    rows_out[1:2, :] = row_total

    def tp_copy(d):
        return pltpu.make_async_remote_copy(
            src_ref=rows_out,
            dst_ref=rows_in.at[n_tp - 1 - d],
            send_sem=send_tp.at[d - 1],
            recv_sem=recv_tp.at[n_tp - 1 - d],
            device_id=(ctx, (tp + d) % n_tp),
            device_id_type=MESH,
        )

    for d in range(1, n_tp):
        tp_copy(d).start()
    for d in range(1, n_tp):
        tp_copy(d).wait_recv()
    sums = rows_out[0:2, :]
    for d in range(n_tp - 1):
        sums = sums + rows_in[d, 0:2, :]
    inv = lax.rsqrt(sums[0:1] / features + EPSILON)
    pull = inv * inv * (sums[1:2] / features)
    for h in range(heads):
        ga = (inv * (w_t[cols(h), :] - att_t[cols(h), :] * pull)).astype(BF16)
        ga_t[cols(h), :] = ga
        put_state(1, h, dot(ga, q[:, cols(h)]))
    scan_start(1)

    obuf[0] = ((att_t[...] * inv).T * gain_ref[...]).astype(BF16)
    outs = [
        pltpu.make_async_copy(obuf.at[j], dst, out_sem.at[j])
        for j, dst in enumerate((normed_hbm, gq_hbm, gk_hbm, gv_hbm))
    ]
    outs[0].start()
    for h in range(heads):
        gv_part[:, cols(h)] = dot_t(scores_t[h], ga_t[cols(h), :])
    scan_middle(1)
    for h in range(heads):
        raw = dot(v[:, cols(h)], ga_t[cols(h), :]) * factor
        gs_t = jnp.where(causal_t, raw, 0.0).astype(BF16)
        gk_part[:, cols(h)] = dot(gs_t, q[:, cols(h)])
        gq = dot(ga_t[cols(h), :].T, state_of(0, h)) * factor + dot(gs_t.T, k[:, cols(h)])
        obuf[1, :, cols(h)] = gq.astype(BF16)
    outs[1].start()
    scan_end(1)
    scan_wait(1)
    for h in range(heads):
        s_t = state_of(1, h)
        gk = dot(v[:, cols(h)], s_t) * factor + gk_part[:, cols(h)]
        obuf[2, :, cols(h)] = gk.astype(BF16)
    outs[2].start()
    for h in range(heads):
        s_t = state_of(1, h)
        gv = dot_t(k[:, cols(h)], s_t) * factor + gv_part[:, cols(h)]
        obuf[3, :, cols(h)] = gv.astype(BF16)
    outs[3].start()

    for i in range(2):
        members_all(i, part, got, send1, recv1).wait_send()
        members_all(i, before, scan_out, send3, recv3).wait_send()
        for other in range(n_groups):

            @pl.when(other > group if i == 0 else other < group)
            def _():
                group_wait(i, other).wait_send()

    for d in range(1, n_tp):
        tp_copy(d).wait_send()
    for out in outs:
        out.wait()


def on_device(n_ctx, n_tp, queries, keys, values, gain, out_grad):
    tokens, width = queries.shape
    heads = width // HEAD
    n_groups = n_ctx // GROUP
    slice_rows = heads * HEAD // GROUP
    tile = jax.ShapeDtypeStruct((tokens, width), BF16)
    hbm = pl.BlockSpec(memory_space=pl.ANY)
    vmem = pltpu.VMEM
    dma = pltpu.SemaphoreType.DMA
    return pl.pallas_call(
        functools.partial(core_kernel, n_ctx, n_tp),
        out_shape=(tile,) * 4,
        in_specs=[hbm, hbm, hbm, pl.BlockSpec(memory_space=pltpu.VMEM), hbm],
        out_specs=(hbm,) * 4,
        scratch_shapes=[
            vmem((tokens, width), BF16),
            vmem((tokens, width), BF16),
            vmem((tokens, width), BF16),
            vmem((tokens, width), BF16),
            vmem((2, GROUP, slice_rows, HEAD), F32),
            vmem((2, GROUP, slice_rows, HEAD), F32),
            vmem((2, slice_rows, HEAD), F32),
            vmem((2, n_groups, slice_rows, HEAD), F32),
            vmem((2, GROUP, slice_rows, HEAD), F32),
            vmem((2, GROUP, slice_rows, HEAD), F32),
            vmem((8, tokens), F32),
            vmem((n_tp - 1, 8, tokens), F32),
            vmem((width, tokens), BF16),
            vmem((width, tokens), BF16),
            vmem((width, tokens), F32),
            vmem((width, tokens), F32),
            vmem((width, tokens), F32),
            vmem((heads, tokens, tokens), BF16),
            vmem((width, tokens), BF16),
            vmem((tokens, width), F32),
            vmem((tokens, width), F32),
            vmem((4, tokens, width), BF16),
            dma((4,)),
            dma((4,)),
            dma((2,)),
            dma((2,)),
            dma((2, n_groups)),
            dma((2, n_groups)),
            dma((2,)),
            dma((2,)),
            dma((n_tp - 1,)),
            dma((n_tp - 1,)),
        ],
        compiler_params=pltpu.CompilerParams(
            collective_id=0, has_side_effects=True, vmem_limit_bytes=32 * 1024 * 1024
        ),
        name="linear_attention",
    )(queries, keys, values, gain.reshape(1, width), out_grad)


def solution(mesh):
    placed = (P("ctx", "tp"), P("ctx", "tp"), P("ctx", "tp"), P("tp"), P("ctx", "tp"))
    return jax.shard_map(
        functools.partial(on_device, mesh.shape["ctx"], mesh.shape["tp"]),
        mesh=mesh,
        in_specs=placed,
        out_specs=(P("ctx", "tp"),) * 4,
        check_vma=False,
    )
```

```python
import functools

import jax
import jax.numpy as jnp
from jax import lax
from jax.experimental import pallas as pl
from jax.experimental.pallas import tpu as pltpu
from jax.sharding import PartitionSpec as P

HEAD = 128
GROUP = 16
EPSILON = 1e-06
MESH = pl.DeviceIdType.MESH
F32 = jnp.float32
BF16 = jnp.bfloat16

STEPS = sorted(
    [(dz, dx, dc) for dz in range(2) for dx in range(4) for dc in range(2) if (dz, dx, dc) != (0, 0, 0)],
    key=lambda s: -(s[0] + min(s[1], 4 - s[1]) + 0.1 * s[2]),
)


def dot(a, b):
    return lax.dot_general(a, b, (((1,), (0,)), ((), ())), preferred_element_type=F32)


def dot_t(a, b):
    return lax.dot_general(a, b, (((1,), (1,)), ((), ())), preferred_element_type=F32)


def core_kernel(
    n_ctx, n_tp,
    q_hbm, k_hbm, v_hbm, gain_hbm, og_hbm,
    normed, gq_out, gk_part, gv_part, k_out, v_out, suffix_out,
    q, k, v, og, gain,
    part, got, total, others, before, scan_out,
    rows_out, rows_in,
    q_t, v_t, w_t, local_t, att_t, scores_t, ga_t,
    in_sem, near_sem, send1, recv1, send2, recv2, send3, recv3, send_tp, recv_tp,
):
    ctx = lax.axis_index("ctx")
    tp = lax.axis_index("tp")
    n_groups = n_ctx // GROUP
    group = ctx // GROUP
    member = ctx % GROUP
    half, x, core = member // 8, (member // 2) % 4, member % 2
    tokens, width = q.shape
    heads = width // HEAD
    slice_rows = part.shape[2]
    factor = (HEAD * tokens * n_ctx) ** (-0.5)
    features = width * n_tp

    pairs = ((k_hbm, k), (v_hbm, v), (q_hbm, q), (og_hbm, og), (gain_hbm, gain))
    loads = [pltpu.make_async_copy(src, dst, in_sem.at[i]) for i, (src, dst) in enumerate(pairs)]
    for load in loads[:2]:
        load.start()
    others[...] = jnp.zeros_like(others)

    def member_at(step):
        dz, dx, dc = step
        return ((half + dz) % 2) * 8 + ((x + dx) % 4) * 2 + (core + dc) % 2

    barrier = pltpu.get_barrier_semaphore()
    greeted = (2, n_groups - 2, 1, n_groups - 1)
    for d in greeted:
        pl.semaphore_signal(
            barrier, inc=1, device_id=(((group + d) % n_groups) * GROUP + member, tp), device_id_type=MESH
        )
    for step in STEPS:
        pl.semaphore_signal(
            barrier, inc=1, device_id=(group * GROUP + member_at(step), tp), device_id_type=MESH
        )
    for d in range(1, n_tp):
        pl.semaphore_signal(barrier, inc=1, device_id=(ctx, (tp + d) % n_tp), device_id_type=MESH)

    for load in loads[2:]:
        load.start()

    row = lax.broadcasted_iota(jnp.int32, (tokens, tokens), 0)
    col = lax.broadcasted_iota(jnp.int32, (tokens, tokens), 1)
    causal_t = row <= col

    def cols(h):
        return pl.ds(h * HEAD, HEAD)

    def put_state(i, h, value):
        per = HEAD // slice_rows
        part[i, h * per:(h + 1) * per] = value.reshape(per, slice_rows, HEAD)

    def state_of(i, h):
        per = HEAD // slice_rows
        return scan_out[i, h * per:(h + 1) * per].reshape(HEAD, HEAD).astype(BF16)

    loads[0].wait()
    loads[1].wait()
    v_t[...] = v[...].T
    for h in range(heads):
        put_state(0, h, dot(v_t[cols(h), :], k[:, cols(h)]))
    loads[2].wait()
    q_t[...] = (q[...].astype(F32) * factor).astype(BF16).T

    pl.semaphore_wait(barrier, (GROUP - 1) + len(greeted) + (n_tp - 1))
    for d in greeted[:2]:
        pl.semaphore_signal(
            near_sem, inc=1, device_id=(((group + d) % n_groups) * GROUP + member, tp), device_id_type=MESH
        )

    def to_members(i, src, dst, send, recv):
        copies = []
        for step in STEPS:
            peer = member_at(step)
            copy = pltpu.make_async_remote_copy(
                src_ref=src.at[i, peer],
                dst_ref=dst.at[i, member],
                send_sem=send.at[i],
                recv_sem=recv.at[i],
                device_id=(group * GROUP + peer, tp),
                device_id_type=MESH,
            )
            copy.start()
            copies.append(copy)
        dst[i, pl.ds(member, 1)] = src[i, pl.ds(member, 1)]

    def members_all(i, src, dst, send, recv):
        most = pl.ds(0, GROUP - 1)
        return pltpu.make_async_remote_copy(
            src_ref=src.at[i, most],
            dst_ref=dst.at[i, most],
            send_sem=send.at[i],
            recv_sem=recv.at[i],
            device_id=(ctx, tp),
            device_id_type=MESH,
        )

    def group_copy(i, other):
        return pltpu.make_async_remote_copy(
            src_ref=total.at[i],
            dst_ref=others.at[i, group],
            send_sem=send2.at[i, other],
            recv_sem=recv2.at[i, group],
            device_id=(other * GROUP + member, tp),
            device_id_type=MESH,
        )

    def group_wait(i, other):
        return pltpu.make_async_remote_copy(
            src_ref=total.at[i],
            dst_ref=others.at[i, other],
            send_sem=send2.at[i, other],
            recv_sem=recv2.at[i, other],
            device_id=(other * GROUP + member, tp),
            device_id_type=MESH,
        )

    def scan_start(i):
        to_members(i, part, got, send1, recv1)

    def scan_middle(i):
        members_all(i, part, got, send1, recv1).wait_recv()
        acc = jnp.zeros((slice_rows, HEAD), F32)
        for s in range(GROUP):
            m = s if i == 0 else GROUP - 1 - s
            before[i, m] = acc
            acc = acc + got[i, m]
        total[i] = acc
        for d in range(n_groups - 1, 0, -1):
            other = group + d if i == 0 else group - d

            @pl.when(other < n_groups if i == 0 else other >= 0)
            def _():
                group_copy(i, other).start()

    def scan_end(i):
        for other in range(n_groups):

            @pl.when(other < group if i == 0 else other > group)
            def _():
                group_wait(i, other).wait_recv()

        carried = others[i, 0]
        for other in range(1, n_groups):
            carried = carried + others[i, other]
        before[i] = before[i] + carried[None]
        to_members(i, before, scan_out, send3, recv3)

    def scan_wait(i):
        members_all(i, before, scan_out, send3, recv3).wait_recv()

    scan_start(0)
    loads[3].wait()
    loads[4].wait()
    w_t[...] = (og[...].astype(F32) * gain[...]).T
    for h in range(heads):
        raw = dot(k[:, cols(h)], q_t[cols(h), :])
        scores_t[h] = jnp.where(causal_t, raw, 0.0).astype(BF16)
    pl.semaphore_wait(near_sem, 2)
    scan_middle(0)
    for h in range(heads):
        local_t[cols(h), :] = dot(v_t[cols(h), :], scores_t[h])
    scan_end(0)
    scan_wait(0)

    power = jnp.zeros((1, tokens), F32)
    row_total = jnp.zeros((1, tokens), F32)
    for h in range(heads):
        att = dot(state_of(0, h), q_t[cols(h), :]) + local_t[cols(h), :]
        att_t[cols(h), :] = att
        power = power + jnp.sum(att * att, axis=0, keepdims=True)
        row_total = row_total + jnp.sum(w_t[cols(h), :] * att, axis=0, keepdims=True)
    rows_out[0:1, :] = power
    rows_out[1:2, :] = row_total

    def tp_copy(d):
        return pltpu.make_async_remote_copy(
            src_ref=rows_out,
            dst_ref=rows_in.at[n_tp - 1 - d],
            send_sem=send_tp.at[d - 1],
            recv_sem=recv_tp.at[n_tp - 1 - d],
            device_id=(ctx, (tp + d) % n_tp),
            device_id_type=MESH,
        )

    for d in range(1, n_tp):
        tp_copy(d).start()
    for d in range(1, n_tp):
        tp_copy(d).wait_recv()
    sums = rows_out[0:2, :]
    for d in range(n_tp - 1):
        sums = sums + rows_in[d, 0:2, :]
    inv = lax.rsqrt(sums[0:1] / features + EPSILON)
    pull = inv * inv * (sums[1:2] / features)
    for h in range(heads):
        ga = (inv * (w_t[cols(h), :] - att_t[cols(h), :] * pull)).astype(BF16)
        ga_t[cols(h), :] = ga
        put_state(1, h, dot(ga, q[:, cols(h)]))
    scan_start(1)

    normed[...] = ((att_t[...] * inv).T * gain[...]).astype(BF16)
    for h in range(heads):
        gv_part[:, cols(h)] = dot_t(scores_t[h], ga_t[cols(h), :])
    scan_middle(1)
    for h in range(heads):
        raw = dot(v[:, cols(h)], ga_t[cols(h), :]) * factor
        gs_t = jnp.where(causal_t, raw, 0.0).astype(BF16)
        gk_part[:, cols(h)] = dot(gs_t, q[:, cols(h)])
        gq = dot(ga_t[cols(h), :].T, state_of(0, h)) * factor + dot(gs_t.T, k[:, cols(h)])
        gq_out[:, cols(h)] = gq.astype(BF16)
    k_out[...] = (k[...].astype(F32) * factor).astype(BF16)
    v_out[...] = (v[...].astype(F32) * factor).astype(BF16)
    scan_end(1)
    scan_wait(1)
    for h in range(heads):
        suffix_out[h * HEAD:(h + 1) * HEAD, :] = state_of(1, h)

    for i in range(2):
        members_all(i, part, got, send1, recv1).wait_send()
        members_all(i, before, scan_out, send3, recv3).wait_send()
        for other in range(n_groups):

            @pl.when(other > group if i == 0 else other < group)
            def _():
                group_wait(i, other).wait_send()

    for d in range(1, n_tp):
        tp_copy(d).wait_send()


def last_kernel(
    normed, gq, gk_part, gv_part, k, v, suffix,
    normed_hbm, gq_hbm, gk_hbm, gv_hbm,
    gk, gv, sem,
):
    heads = suffix.shape[0] // HEAD
    outs = [
        pltpu.make_async_copy(src, dst, sem.at[j])
        for j, (src, dst) in enumerate(((normed, normed_hbm), (gq, gq_hbm), (gk, gk_hbm), (gv, gv_hbm)))
    ]
    outs[0].start()
    outs[1].start()
    for h in range(heads):
        cols = pl.ds(h * HEAD, HEAD)
        gk[:, cols] = (dot(v[:, cols], suffix[cols, :]) + gk_part[:, cols]).astype(BF16)
    outs[2].start()
    for h in range(heads):
        cols = pl.ds(h * HEAD, HEAD)
        gv[:, cols] = (dot_t(k[:, cols], suffix[cols, :]) + gv_part[:, cols]).astype(BF16)
    outs[3].start()
    for out in outs:
        out.wait()


def on_device(n_ctx, n_tp, queries, keys, values, gain, out_grad):
    tokens, width = queries.shape
    heads = width // HEAD
    n_groups = n_ctx // GROUP
    slice_rows = heads * HEAD // GROUP
    hbm = pl.BlockSpec(memory_space=pl.ANY)
    inside = pl.BlockSpec(memory_space=pltpu.VMEM)
    vmem = pltpu.VMEM
    dma = pltpu.SemaphoreType.DMA
    args = [
        pltpu.with_memory_space_constraint(a, pltpu.HBM)
        for a in (queries, keys, values, gain.reshape(1, width), out_grad)
    ]
    half = pltpu.VMEM((tokens, width), BF16)
    full = pltpu.VMEM((tokens, width), F32)
    held = pl.pallas_call(
        functools.partial(core_kernel, n_ctx, n_tp),
        out_shape=(half, half, full, full, half, half, pltpu.VMEM((width, HEAD), BF16)),
        in_specs=[hbm] * 5,
        out_specs=(inside,) * 7,
        scratch_shapes=[
            vmem((tokens, width), BF16),
            vmem((tokens, width), BF16),
            vmem((tokens, width), BF16),
            vmem((tokens, width), BF16),
            vmem((1, width), F32),
            vmem((2, GROUP, slice_rows, HEAD), F32),
            vmem((2, GROUP, slice_rows, HEAD), F32),
            vmem((2, slice_rows, HEAD), F32),
            vmem((2, n_groups, slice_rows, HEAD), F32),
            vmem((2, GROUP, slice_rows, HEAD), F32),
            vmem((2, GROUP, slice_rows, HEAD), F32),
            vmem((8, tokens), F32),
            vmem((n_tp - 1, 8, tokens), F32),
            vmem((width, tokens), BF16),
            vmem((width, tokens), BF16),
            vmem((width, tokens), F32),
            vmem((width, tokens), F32),
            vmem((width, tokens), F32),
            vmem((heads, tokens, tokens), BF16),
            vmem((width, tokens), BF16),
            dma((5,)),
            pltpu.SemaphoreType.REGULAR,
            dma((2,)),
            dma((2,)),
            dma((2, n_groups)),
            dma((2, n_groups)),
            dma((2,)),
            dma((2,)),
            dma((n_tp - 1,)),
            dma((n_tp - 1,)),
        ],
        compiler_params=pltpu.CompilerParams(
            collective_id=0, has_side_effects=True, vmem_limit_bytes=32 * 1024 * 1024
        ),
        name="linear_attention",
    )(*args)
    held = [pltpu.with_memory_space_constraint(a, pltpu.VMEM) for a in held]
    return pl.pallas_call(
        last_kernel,
        out_shape=(pltpu.HBM((tokens, width), BF16),) * 4,
        in_specs=[inside] * 7,
        out_specs=(hbm,) * 4,
        scratch_shapes=[
            vmem((tokens, width), BF16),
            vmem((tokens, width), BF16),
            dma((4,)),
        ],
        compiler_params=pltpu.CompilerParams(vmem_limit_bytes=16 * 1024 * 1024),
        name="last_products",
    )(*held)


def solution(mesh):
    placed = (P("ctx", "tp"), P("ctx", "tp"), P("ctx", "tp"), P("tp"), P("ctx", "tp"))
    return jax.shard_map(
        functools.partial(on_device, mesh.shape["ctx"], mesh.shape["tp"]),
        mesh=mesh,
        in_specs=placed,
        out_specs=(P("ctx", "tp"),) * 4,
        check_vma=False,
    )
```
